32 devices in a mesh: blk: 4 (over z), uly: 8 (over y, x, core).
Axes of the slice: x: 2, y: 2, z: 4, core: 2. Of those that a mesh axis runs over, the one named last changes fastest.
Arguments:
- video_q: bfloat16 [4096, 2048], P(('blk', 'uly')), may hold values from -100 to 100
- video_k: bfloat16 [4096, 2048], P(('blk', 'uly')), may hold values from -100 to 100
- video_v: bfloat16 [4096, 2048], P(('blk', 'uly')), may hold values from -6 to 6
- text_q: bfloat16 [256, 2048], replicated, may hold values from -100 to 100
- text_k: bfloat16 [256, 2048], replicated, may hold values from -100 to 100
- text_v: bfloat16 [256, 2048], replicated, may hold values from -6 to 6
Outputs:
- video_out: bfloat16 [4096, 2048], P(('blk', 'uly'))
- text_out: bfloat16 [256, 2048], P(('blk', 'uly'))
The draws below stay inside these ranges and needn't reach their ends.
All inputs are finite; a program needn't handle non-finite values.
Results may differ from the reference program's by a relative error of at most 0.0039.
Values may be sent and summed in bfloat16 or wider, within the bound.
A program may use at most 128 MiB of HBM per device.

```python
import jax
import jax.numpy as jnp
from jax import lax

HEADS = 16
HEAD_DIM = 128
TEXT = 256
TOKENS = 4096


def raw_field(key, rows):
    return 1.6 * jax.random.truncated_normal(key, -5.0, 5.0, (rows, HEADS * HEAD_DIM), jnp.float32)


def draw_video_k(key, part):
    shared = raw_field(jax.random.fold_in(key, 202), TOKENS)
    return shared.astype(jnp.bfloat16)


def draw_video_q(key, part):
    key = jax.random.fold_in(key, 7)
    return raw_field(key, TOKENS).astype(jnp.bfloat16)


def draw_text_k(key, part):
    shared = raw_field(jax.random.fold_in(key, 101), TEXT)
    return shared.astype(jnp.bfloat16)


def draw_text_q(key, part):
    key = jax.random.fold_in(key, 9)
    return raw_field(key, TEXT).astype(jnp.bfloat16)


def level_of(stream_key, extent, pieces, least, high):
    gain, own = 1.0, jax.random.fold_in(stream_key, 6)
    for position, parts in pieces:
        draws = jnp.exp(jax.random.uniform(jax.random.fold_in(own, position), (parts,), jnp.float32, least / len(pieces), high / len(pieces)))
        gain = gain * jnp.repeat(draws, extent[position] // parts).reshape([-1 if axis == position else 1 for axis in range(len(extent))])
    return gain


def scatter_about(rng, dims, scale, bound, shards=(), held_as=jnp.bfloat16):
    loudness = level_of(rng, dims, shards, -0.22, 0.18) if shards else 1.0
    values = jax.random.normal(rng, dims, jnp.float32) * scale * loudness
    return jnp.minimum(jnp.maximum(values, -bound), bound).astype(held_as)


def setup_inputs(seed: int = 0) -> dict:
    splits = jax.random.split(jax.random.key(seed), 7)
    return {
        "video_q": draw_video_q(jax.random.fold_in(splits[6], 71), 0),
        "video_k": draw_video_k(jax.random.fold_in(splits[6], 71), 0),
        "video_v": scatter_about(splits[2], (TOKENS, HEADS * HEAD_DIM), 1.0, 6.0, ((0, 32),)),
        "text_q": draw_text_q(jax.random.fold_in(splits[6], 71), 0),
        "text_k": draw_text_k(jax.random.fold_in(splits[6], 71), 0),
        "text_v": scatter_about(splits[5], (TEXT, HEADS * HEAD_DIM), 1.0, 6.0),
    }


def reference(video_q, video_k, video_v, text_q, text_k, text_v):
    queries = jnp.concatenate([video_q, text_q], axis=0)
    key_all = jnp.concatenate([video_k, text_k], axis=0)
    value_all = jnp.concatenate([video_v, text_v], axis=0)
    joint_rows = TOKENS + TEXT
    block_rows = joint_rows // 8
    score_scale = HEAD_DIM ** -0.5

    def one_head(head_index):
        column = head_index * HEAD_DIM
        query_head = lax.dynamic_slice_in_dim(queries, column, HEAD_DIM, 1)
        key_head = lax.dynamic_slice_in_dim(key_all, column, HEAD_DIM, 1)
        value_head = lax.dynamic_slice_in_dim(value_all, column, HEAD_DIM, 1)

        def one_block(row_start):
            query_block = lax.dynamic_slice_in_dim(query_head, row_start, block_rows, 0)
            scores = jnp.dot(query_block, key_head.T, preferred_element_type=jnp.float32) * score_scale
            top_score = jnp.max(scores, axis=1, keepdims=True)
            raised = jnp.exp(scores - top_score)
            denominator = jnp.sum(raised, axis=1, keepdims=True)
            weights = raised.astype(jnp.bfloat16)
            numerator = jnp.dot(weights, value_head, preferred_element_type=jnp.float32)
            return (numerator / denominator).astype(jnp.bfloat16)

        starts = jnp.arange(8, dtype=jnp.int32) * block_rows
        return lax.map(one_block, starts).reshape(joint_rows, HEAD_DIM)

    per_head = lax.map(one_head, jnp.arange(HEADS, dtype=jnp.int32))
    attended = jnp.transpose(per_head, (1, 0, 2)).reshape(joint_rows, HEADS * HEAD_DIM)
    return attended[:TOKENS], attended[TOKENS:]
```

```python
import functools
import math

import jax
import jax.numpy as jnp
from jax import lax
from jax.experimental import pallas as pl
from jax.experimental.pallas import tpu as pltpu
from jax.sharding import PartitionSpec as P

HEAD_DIM = 128
CORES = 2
MESH = pl.DeviceIdType.MESH
EXPONENT_SCALE = HEAD_DIM ** (-0.5) * math.log2(math.e)


def chunk_bounds(total, width):
    count = max(total // width, 1)
    starts = [i * width for i in range(count)]
    return [(s, (total if i == count - 1 else starts[i + 1]) - s) for i, s in enumerate(starts)]


def score(queries, keys):
    return lax.dot_general(
        queries, keys, (((1,), (1,)), ((), ())), preferred_element_type=jnp.float32
    )


def weigh(raised, values):
    ones = jnp.ones(values.shape, values.dtype)
    return jnp.dot(
        raised, jnp.concatenate([values, ones], axis=1), preferred_element_type=jnp.float32
    )


def attend(queries, k_ref, v_ref, key_width):
    rows = queries.shape[0]
    key_count = k_ref.shape[0]

    def absorb(state, keys, values):
        top, total = state
        scores = score(queries, keys)
        part_top = jnp.max(scores, axis=1, keepdims=True)
        new_top = part_top if top is None else jnp.maximum(top, part_top)
        raised = jnp.exp2((scores - new_top) * EXPONENT_SCALE)
        part = weigh(raised.astype(jnp.bfloat16), values)
        if top is not None:
            part = total * jnp.exp2((top - new_top) * EXPONENT_SCALE) + part
        return new_top, part

    bounds = chunk_bounds(key_count, key_width)
    if len(bounds) <= 8:
        state = (None, None)
        for start, width in bounds:
            state = absorb(
                state, k_ref[start : start + width, :], v_ref[start : start + width, :]
            )
    else:
        start, width = bounds[-1]
        state = absorb(
            (None, None), k_ref[start : start + width, :], v_ref[start : start + width, :]
        )

        def step(index, state):
            rows_here = pl.ds(pl.multiple_of(index * key_width, key_width), key_width)
            return absorb(state, k_ref[rows_here, :], v_ref[rows_here, :])

        state = lax.fori_loop(0, len(bounds) - 1, step, state)
    total = state[1]
    return total[:, :HEAD_DIM] / total[:, HEAD_DIM:]


def kernel(
    blk_count, uly_count, key_width, group,
    vq, vk, vv, tq, tk, tv, vout, tout,
    kbuf, vbuf, qbuf, obuf, tqbuf, tsend, tin,
    local_sem, k_send, k_recv, v_send, v_recv, kf_send, kf_recv, vf_send, vf_recv,
    q_send, q_recv, o_send, o_recv, t_send, t_recv,
):
    rows = vq.shape[0]
    heads = vq.shape[1] // HEAD_DIM
    text = tq.shape[0]
    chips = blk_count * uly_count // CORES
    video_keys = chips * CORES * rows
    text_each = text // (chips * CORES)
    me = lax.axis_index("blk") * uly_count + lax.axis_index("uly")
    core = lax.rem(me, CORES)
    chip = me // CORES
    head = lax.rem(chip, heads)
    base = chip - head

    def device(to_chip, to_core):
        index = to_chip * CORES + to_core
        return (index // uly_count, lax.rem(index, uly_count))

    def columns(index):
        return pl.ds(pl.multiple_of(index * HEAD_DIM, HEAD_DIM), HEAD_DIM)

    def slot(k, of_core):
        return pl.ds(pl.multiple_of((k * CORES + of_core) * rows, rows), rows)

    def row_block(k):
        return pl.ds(pl.multiple_of(k * rows, rows), rows)

    def remote(src, dst, send, recv, target):
        return pltpu.make_async_remote_copy(
            src_ref=src, dst_ref=dst, send_sem=send, recv_sem=recv,
            device_id=target, device_id_type=MESH,
        )

    def kv_copies(k):
        to = lax.rem(chip + k, chips)
        where = columns(lax.rem(to, heads))
        return (
            remote(vk.at[:, where], kbuf.at[slot(k, core), :], k_send.at[k], k_recv.at[k], device(to, core)),
            remote(vv.at[:, where], vbuf.at[slot(k, core), :], v_send.at[k], v_recv.at[k], device(to, core)),
        )

    def forward_copies(k, of_core):
        part = slot(k, of_core)
        return (
            remote(kbuf.at[part, :], kbuf.at[part, :], kf_send.at[k], kf_recv.at[k], device(chip, 1 - core)),
            remote(vbuf.at[part, :], vbuf.at[part, :], vf_send.at[k], vf_recv.at[k], device(chip, 1 - core)),
        )

    def q_copy(k):
        to = lax.rem(head + k, heads)
        return remote(
            vq.at[:, columns(to)], qbuf.at[row_block(k), :], q_send.at[k], q_recv.at[k],
            device(base + to, core),
        )

    def o_copy(k):
        to = lax.rem(head - k + heads, heads)
        return remote(
            obuf.at[row_block(k), :], vout.at[:, columns(head)], o_send.at[k], o_recv.at[k],
            device(base + to, core),
        )

    def t_copy(k):
        to = lax.rem(head - k + heads, heads)
        return remote(tsend.at[k], tin.at[head], t_send.at[k], t_recv.at[k], device(base + to, core))

    text_rows = pl.ds(video_keys, text)
    own = [
        pltpu.make_async_copy(vk.at[:, columns(head)], kbuf.at[slot(0, core), :], local_sem.at[0]),
        pltpu.make_async_copy(vv.at[:, columns(head)], vbuf.at[slot(0, core), :], local_sem.at[1]),
        pltpu.make_async_copy(vq.at[:, columns(head)], qbuf.at[row_block(0), :], local_sem.at[2]),
        pltpu.make_async_copy(tq.at[:, columns(head)], tqbuf, local_sem.at[3]),
        pltpu.make_async_copy(tk.at[:, columns(head)], kbuf.at[text_rows, :], local_sem.at[4]),
        pltpu.make_async_copy(tv.at[:, columns(head)], vbuf.at[text_rows, :], local_sem.at[5]),
    ]
    for copy in own:
        copy.start()

    barrier = pltpu.get_barrier_semaphore()

    def greet(k, _):
        pl.semaphore_signal(
            barrier, inc=1, device_id=device(lax.rem(chip + k, chips), core), device_id_type=MESH
        )
        return 0

    lax.fori_loop(1, chips, greet, 0)
    pl.semaphore_signal(barrier, inc=1, device_id=device(chip, 1 - core), device_id_type=MESH)
    pl.semaphore_wait(barrier, chips)

    def send_kv(k, _):
        for copy in kv_copies(k):
            copy.start()
        return 0

    lax.fori_loop(1, chips, send_kv, 0)
    for copy in own:
        copy.wait()
    for copy in forward_copies(0, core):
        copy.start()

    def hand_on(k, _):
        for copy in kv_copies(k):
            copy.wait_recv()
        for copy in forward_copies(k, core):
            copy.start()
        if chips == heads:
            q_copy(k).start()
        else:
            pl.when(k < heads)(lambda: q_copy(k).start())
        return 0

    lax.fori_loop(1, chips, hand_on, 0)

    picked = heads * text_each
    shift = text_each.bit_length() - 1
    row = lax.broadcasted_iota(jnp.int32, (picked, text), 0)
    source = lax.broadcasted_iota(jnp.int32, (picked, text), 1)
    k_of = lax.shift_right_logical(row, shift)
    owner = head - k_of
    owner = base + jnp.where(owner < 0, owner + heads, owner)
    wanted = (owner * CORES + core) * text_each + (row - k_of * text_each)
    pick = jnp.where(source == wanted, 1.0, 0.0).astype(jnp.bfloat16)
    text_queries = jnp.dot(pick, tqbuf[...], preferred_element_type=jnp.float32).astype(jnp.bfloat16)

    def arrive(k, _):
        for copy in forward_copies(k, 1 - core):
            copy.wait_recv()
        return 0

    lax.fori_loop(0, chips, arrive, 0)

    attended = attend(text_queries, kbuf, vbuf, key_width)
    for k in range(heads):
        tsend[k, 0:text_each, :] = attended[k * text_each : (k + 1) * text_each, :]

    def send_text(k, _):
        t_copy(k).start()
        return 0

    lax.fori_loop(1, heads, send_text, 0)
    tin[head, :, :] = tsend[0, :, :]

    home = pltpu.make_async_copy(obuf.at[row_block(0), :], vout.at[:, columns(head)], local_sem.at[0])

    def block(b, _):
        for i in range(group):
            k = b * group + i
            if i == 0:
                pl.when(k > 0)(lambda: q_copy(k).wait_recv())
            else:
                q_copy(k).wait_recv()
        here = pl.ds(pl.multiple_of(b * group * rows, group * rows), group * rows)
        obuf[here, :] = attend(qbuf[here, :], kbuf, vbuf, key_width).astype(jnp.bfloat16)
        for i in range(group):
            k = b * group + i
            if i == 0:
                pl.when(k > 0)(lambda: o_copy(k).start())
                pl.when(k == 0)(lambda: home.start())
            else:
                o_copy(k).start()
        return 0

    lax.fori_loop(0, heads // group, block, 0)

    def finish(k, _):
        t_copy(k).wait()
        q_copy(k).wait_send()
        return 0

    lax.fori_loop(1, heads, finish, 0)
    for h in range(heads):
        tout[:, h * HEAD_DIM : (h + 1) * HEAD_DIM] = tin[h, 0:text_each, :].astype(jnp.bfloat16)
    home.wait()

    def finish_kv(k, _):
        for copy in kv_copies(k) + forward_copies(k, core):
            copy.wait_send()
        return 0

    for copy in forward_copies(0, core):
        copy.wait_send()
    lax.fori_loop(1, chips, finish_kv, 0)

    def finish_o(k, _):
        o_copy(k).wait()
        return 0

    lax.fori_loop(1, heads, finish_o, 0)


def per_device(blk_count, uly_count, video_q, video_k, video_v, text_q, text_k, text_v):
    rows, width = video_q.shape
    heads = width // HEAD_DIM
    text = text_q.shape[0]
    chips = blk_count * uly_count // CORES
    keys = chips * CORES * rows + text
    text_each = text // (chips * CORES)
    tile = max(text_each, 8)
    flops = 4 * (heads * rows + heads * text_each) * keys * HEAD_DIM
    dma = pltpu.SemaphoreType.DMA
    any_space = pl.BlockSpec(memory_space=pl.ANY)
    return pl.pallas_call(
        functools.partial(kernel, blk_count, uly_count, 1024, 2),
        out_shape=(
            jax.ShapeDtypeStruct((rows, width), jnp.bfloat16),
            jax.ShapeDtypeStruct((text_each, width), jnp.bfloat16),
        ),
        in_specs=[any_space] * 6,
        out_specs=(any_space, pl.BlockSpec(memory_space=pltpu.VMEM)),
        scratch_shapes=[
            pltpu.VMEM((keys, HEAD_DIM), jnp.bfloat16),
            pltpu.VMEM((keys, HEAD_DIM), jnp.bfloat16),
            pltpu.VMEM((heads * rows, HEAD_DIM), jnp.bfloat16),
            pltpu.VMEM((heads * rows, HEAD_DIM), jnp.bfloat16),
            pltpu.VMEM((text, HEAD_DIM), jnp.bfloat16),
            pltpu.VMEM((heads, tile, HEAD_DIM), jnp.float32),
            pltpu.VMEM((heads, tile, HEAD_DIM), jnp.float32),
            dma((6,)),
        ]
        + [dma((chips,))] * 8
        + [dma((heads,))] * 6,
        compiler_params=pltpu.CompilerParams(
            collective_id=0, has_side_effects=True, vmem_limit_bytes=56 * 1024 * 1024
        ),
        cost_estimate=pl.CostEstimate(
            flops=flops, bytes_accessed=8 * rows * width * 2, transcendentals=flops // (4 * HEAD_DIM)
        ),
    )(video_q, video_k, video_v, text_q, text_k, text_v)


def solution(mesh):
    rows = P(("blk", "uly"), None)
    return jax.shard_map(
        functools.partial(per_device, mesh.shape["blk"], mesh.shape["uly"]),
        mesh=mesh,
        in_specs=(rows, rows, rows, P(), P(), P()),
        out_specs=(rows, rows),
        check_vma=False,
    )
```

```python
import functools
import math

import jax
import jax.numpy as jnp
from jax import lax
from jax.experimental import pallas as pl
from jax.experimental.pallas import tpu as pltpu
from jax.sharding import PartitionSpec as P

HEAD_DIM = 128
CORES = 2
MESH = pl.DeviceIdType.MESH
EXPONENT_SCALE = HEAD_DIM ** (-0.5) * math.log2(math.e)


def chunk_bounds(total, width):
    count = max(total // width, 1)
    starts = [i * width for i in range(count)]
    return [(s, (total if i == count - 1 else starts[i + 1]) - s) for i, s in enumerate(starts)]


def pair(a, b, count):
    total, bit = 0, 1
    while bit < count:
        total = total + lax.rem(a // bit + b // bit, 2) * bit
        bit *= 2
    return total


def score(queries, keys):
    return lax.dot_general(
        queries, keys, (((1,), (1,)), ((), ())), preferred_element_type=jnp.float32
    )


def weigh(raised, values):
    ones = jnp.ones(values.shape, values.dtype)
    return jnp.dot(
        raised, jnp.concatenate([values, ones], axis=1), preferred_element_type=jnp.float32
    )


def attend(queries, k_ref, v_ref, key_width):
    rows = queries.shape[0]
    key_count = k_ref.shape[0]

    def absorb(state, keys, values):
        top, total = state
        scores = score(queries, keys)
        part_top = jnp.max(scores, axis=1, keepdims=True)
        new_top = part_top if top is None else jnp.maximum(top, part_top)
        raised = jnp.exp2((scores - new_top) * EXPONENT_SCALE)
        part = weigh(raised.astype(jnp.bfloat16), values)
        if top is not None:
            part = total * jnp.exp2((top - new_top) * EXPONENT_SCALE) + part
        return new_top, part

    bounds = chunk_bounds(key_count, key_width)
    if len(bounds) <= 8:
        state = (None, None)
        for start, width in bounds:
            state = absorb(
                state, k_ref[start : start + width, :], v_ref[start : start + width, :]
            )
    else:
        start, width = bounds[-1]
        state = absorb(
            (None, None), k_ref[start : start + width, :], v_ref[start : start + width, :]
        )

        def step(index, state):
            rows_here = pl.ds(pl.multiple_of(index * key_width, key_width), key_width)
            return absorb(state, k_ref[rows_here, :], v_ref[rows_here, :])

        state = lax.fori_loop(0, len(bounds) - 1, step, state)
    total = state[1]
    return total[:, :HEAD_DIM] / total[:, HEAD_DIM:]


def kernel(
    blk_count, uly_count, key_width, group,
    vq, vk, vv, tq, tk, tv, vout, tout,
    kbuf, vbuf, qbuf, obuf, tqbuf, tsend, tin,
    local_sem, k_send, k_recv, v_send, v_recv, kf_send, kf_recv, vf_send, vf_recv,
    q_send, q_recv, o_send, o_recv, t_send, t_recv,
):
    rows = vq.shape[0]
    heads = vq.shape[1] // HEAD_DIM
    text = tq.shape[0]
    chips = blk_count * uly_count // CORES
    video_keys = chips * CORES * rows
    text_each = text // (chips * CORES)
    me = lax.axis_index("blk") * uly_count + lax.axis_index("uly")
    core = lax.rem(me, CORES)
    chip = me // CORES
    head = lax.rem(chip, heads)
    base = chip - head

    def device(to_chip, to_core):
        index = to_chip * CORES + to_core
        return (index // uly_count, lax.rem(index, uly_count))

    def columns(index):
        return pl.ds(pl.multiple_of(index * HEAD_DIM, HEAD_DIM), HEAD_DIM)

    def slot(k, of_core):
        return pl.ds(pl.multiple_of((k * CORES + of_core) * rows, rows), rows)

    def row_block(k):
        return pl.ds(pl.multiple_of(k * rows, rows), rows)

    def remote(src, dst, send, recv, target):
        return pltpu.make_async_remote_copy(
            src_ref=src, dst_ref=dst, send_sem=send, recv_sem=recv,
            device_id=target, device_id_type=MESH,
        )

    def kv_copies(k):
        to = pair(chip, k, chips)
        where = columns(lax.rem(to, heads))
        return (
            remote(vk.at[:, where], kbuf.at[slot(k, core), :], k_send.at[k], k_recv.at[k], device(to, core)),
            remote(vv.at[:, where], vbuf.at[slot(k, core), :], v_send.at[k], v_recv.at[k], device(to, core)),
        )

    def forward_copies(k, of_core):
        part = slot(k, of_core)
        return (
            remote(kbuf.at[part, :], kbuf.at[part, :], kf_send.at[k], kf_recv.at[k], device(chip, 1 - core)),
            remote(vbuf.at[part, :], vbuf.at[part, :], vf_send.at[k], vf_recv.at[k], device(chip, 1 - core)),
        )

    def q_copy(k):
        to = pair(head, k, heads)
        return remote(
            vq.at[:, columns(to)], qbuf.at[row_block(k), :], q_send.at[k], q_recv.at[k],
            device(base + to, core),
        )

    def o_copy(k):
        to = pair(head, k, heads)
        return remote(
            obuf.at[row_block(k), :], vout.at[:, columns(head)], o_send.at[k], o_recv.at[k],
            device(base + to, core),
        )

    def t_copy(k):
        to = pair(head, k, heads)
        return remote(tsend.at[k], tin.at[head], t_send.at[k], t_recv.at[k], device(base + to, core))

    text_rows = pl.ds(video_keys, text)
    own = [
        pltpu.make_async_copy(vk.at[:, columns(head)], kbuf.at[slot(0, core), :], local_sem.at[0]),
        pltpu.make_async_copy(vv.at[:, columns(head)], vbuf.at[slot(0, core), :], local_sem.at[1]),
        pltpu.make_async_copy(vq.at[:, columns(head)], qbuf.at[row_block(0), :], local_sem.at[2]),
        pltpu.make_async_copy(tq.at[:, columns(head)], tqbuf, local_sem.at[3]),
        pltpu.make_async_copy(tk.at[:, columns(head)], kbuf.at[text_rows, :], local_sem.at[4]),
        pltpu.make_async_copy(tv.at[:, columns(head)], vbuf.at[text_rows, :], local_sem.at[5]),
    ]
    for copy in own:
        copy.start()

    barrier = pltpu.get_barrier_semaphore()

    def greet(k, _):
        pl.semaphore_signal(
            barrier, inc=1, device_id=device(pair(chip, k, chips), core), device_id_type=MESH
        )
        return 0

    lax.fori_loop(1, chips, greet, 0)
    pl.semaphore_signal(barrier, inc=1, device_id=device(chip, 1 - core), device_id_type=MESH)
    pl.semaphore_wait(barrier, chips)

    def send_kv(j, _):
        k = chips - j
        for copy in kv_copies(k):
            copy.start()
        return 0

    lax.fori_loop(1, chips, send_kv, 0)
    for copy in own:
        copy.wait()
    for copy in forward_copies(0, core):
        copy.start()

    def hand_on(j, _):
        k = chips - j
        for copy in kv_copies(k):
            copy.wait_recv()
        for copy in forward_copies(k, core):
            copy.start()
        if chips == heads:
            q_copy(k).start()
        else:
            pl.when(k < heads)(lambda: q_copy(k).start())
        return 0

    lax.fori_loop(1, chips, hand_on, 0)

    picked = heads * text_each
    shift = text_each.bit_length() - 1
    row = lax.broadcasted_iota(jnp.int32, (picked, text), 0)
    source = lax.broadcasted_iota(jnp.int32, (picked, text), 1)
    k_of = lax.shift_right_logical(row, shift)
    owner = base + lax.bitwise_xor(jnp.full_like(k_of, head), k_of)
    wanted = (owner * CORES + core) * text_each + (row - k_of * text_each)
    pick = jnp.where(source == wanted, 1.0, 0.0).astype(jnp.bfloat16)
    text_queries = jnp.dot(pick, tqbuf[...], preferred_element_type=jnp.float32).astype(jnp.bfloat16)

    def arrive(k, _):
        for copy in forward_copies(k, 1 - core):
            copy.wait_recv()
        return 0

    lax.fori_loop(0, chips, arrive, 0)

    attended = attend(text_queries, kbuf, vbuf, key_width)
    for k in range(heads):
        tsend[k, 0:text_each, :] = attended[k * text_each : (k + 1) * text_each, :]

    def send_text(k, _):
        t_copy(k).start()
        return 0

    lax.fori_loop(1, heads, send_text, 0)
    tin[head, :, :] = tsend[0, :, :]

    home = pltpu.make_async_copy(obuf.at[row_block(0), :], vout.at[:, columns(head)], local_sem.at[0])

    def block(step, _):
        b = heads // group - 1 - step
        for i in range(group):
            k = b * group + i
            if i == 0:
                pl.when(k > 0)(lambda: q_copy(k).wait_recv())
            else:
                q_copy(k).wait_recv()
        here = pl.ds(pl.multiple_of(b * group * rows, group * rows), group * rows)
        obuf[here, :] = attend(qbuf[here, :], kbuf, vbuf, key_width).astype(jnp.bfloat16)
        for i in range(group):
            k = b * group + i
            if i == 0:
                pl.when(k > 0)(lambda: o_copy(k).start())
                pl.when(k == 0)(lambda: home.start())
            else:
                o_copy(k).start()
        return 0

    lax.fori_loop(0, heads // group, block, 0)

    def finish(k, _):
        t_copy(k).wait()
        q_copy(k).wait_send()
        return 0

    lax.fori_loop(1, heads, finish, 0)
    for h in range(heads):
        tout[:, h * HEAD_DIM : (h + 1) * HEAD_DIM] = tin[h, 0:text_each, :].astype(jnp.bfloat16)
    home.wait()

    def finish_kv(k, _):
        for copy in kv_copies(k) + forward_copies(k, core):
            copy.wait_send()
        return 0

    for copy in forward_copies(0, core):
        copy.wait_send()
    lax.fori_loop(1, chips, finish_kv, 0)

    def finish_o(k, _):
        o_copy(k).wait()
        return 0

    lax.fori_loop(1, heads, finish_o, 0)


def per_device(blk_count, uly_count, video_q, video_k, video_v, text_q, text_k, text_v):
    rows, width = video_q.shape
    heads = width // HEAD_DIM
    text = text_q.shape[0]
    chips = blk_count * uly_count // CORES
    keys = chips * CORES * rows + text
    text_each = text // (chips * CORES)
    tile = max(text_each, 8)
    flops = 4 * (heads * rows + heads * text_each) * keys * HEAD_DIM
    dma = pltpu.SemaphoreType.DMA
    any_space = pl.BlockSpec(memory_space=pl.ANY)
    return pl.pallas_call(
        functools.partial(kernel, blk_count, uly_count, 2176, 4),
        out_shape=(
            jax.ShapeDtypeStruct((rows, width), jnp.bfloat16),
            jax.ShapeDtypeStruct((text_each, width), jnp.bfloat16),
        ),
        in_specs=[any_space] * 6,
        out_specs=(any_space, pl.BlockSpec(memory_space=pltpu.VMEM)),
        scratch_shapes=[
            pltpu.VMEM((keys, HEAD_DIM), jnp.bfloat16),
            pltpu.VMEM((keys, HEAD_DIM), jnp.bfloat16),
            pltpu.VMEM((heads * rows, HEAD_DIM), jnp.bfloat16),
            pltpu.VMEM((heads * rows, HEAD_DIM), jnp.bfloat16),
            pltpu.VMEM((text, HEAD_DIM), jnp.bfloat16),
            pltpu.VMEM((heads, tile, HEAD_DIM), jnp.float32),
            pltpu.VMEM((heads, tile, HEAD_DIM), jnp.float32),
            dma((6,)),
        ]
        + [dma((chips,))] * 8
        + [dma((heads,))] * 6,
        compiler_params=pltpu.CompilerParams(
            collective_id=0, has_side_effects=True, vmem_limit_bytes=56 * 1024 * 1024
        ),
        cost_estimate=pl.CostEstimate(
            flops=flops, bytes_accessed=8 * rows * width * 2, transcendentals=flops // (4 * HEAD_DIM)
        ),
    )(video_q, video_k, video_v, text_q, text_k, text_v)


def solution(mesh):
    rows = P(("blk", "uly"), None)
    return jax.shard_map(
        functools.partial(per_device, mesh.shape["blk"], mesh.shape["uly"]),
        mesh=mesh,
        in_specs=(rows, rows, rows, P(), P(), P()),
        out_specs=(rows, rows),
        check_vma=False,
    )
```

```python
import functools
import math

import jax
import jax.numpy as jnp
from jax import lax
from jax.experimental import pallas as pl
from jax.experimental.pallas import tpu as pltpu
from jax.sharding import PartitionSpec as P

HEAD_DIM = 128
CORES = 2
MESH = pl.DeviceIdType.MESH
EXPONENT_SCALE = HEAD_DIM ** (-0.5) * math.log2(math.e)


def chunk_bounds(total, width):
    count = max(total // width, 1)
    starts = [i * width for i in range(count)]
    return [(s, (total if i == count - 1 else starts[i + 1]) - s) for i, s in enumerate(starts)]


def pair(a, b, count):
    total, bit = 0, 1
    while bit < count:
        total = total + lax.rem(a // bit + b // bit, 2) * bit
        bit *= 2
    return total


def score(queries, keys):
    return lax.dot_general(
        queries, keys, (((1,), (1,)), ((), ())), preferred_element_type=jnp.float32
    )


def weigh(raised, values):
    ones = jnp.ones(values.shape, values.dtype)
    return jnp.dot(
        raised, jnp.concatenate([values, ones], axis=1), preferred_element_type=jnp.float32
    )


def attend(queries, k_ref, v_ref, key_width):
    rows = queries.shape[0]
    key_count = k_ref.shape[0]

    def absorb(state, keys, values):
        top, total = state
        scores = score(queries, keys)
        part_top = jnp.max(scores, axis=1, keepdims=True)
        new_top = part_top if top is None else jnp.maximum(top, part_top)
        raised = jnp.exp2((scores - new_top) * EXPONENT_SCALE)
        part = weigh(raised.astype(jnp.bfloat16), values)
        if top is not None:
            part = total * jnp.exp2((top - new_top) * EXPONENT_SCALE) + part
        return new_top, part

    bounds = chunk_bounds(key_count, key_width)
    if len(bounds) <= 8:
        state = (None, None)
        for start, width in bounds:
            state = absorb(
                state, k_ref[start : start + width, :], v_ref[start : start + width, :]
            )
    else:
        start, width = bounds[-1]
        state = absorb(
            (None, None), k_ref[start : start + width, :], v_ref[start : start + width, :]
        )

        def step(index, state):
            rows_here = pl.ds(pl.multiple_of(index * key_width, key_width), key_width)
            return absorb(state, k_ref[rows_here, :], v_ref[rows_here, :])

        state = lax.fori_loop(0, len(bounds) - 1, step, state)
    total = state[1]
    return total[:, :HEAD_DIM] / total[:, HEAD_DIM:]


def kernel(
    blk_count, uly_count, key_width, group,
    vq, vk, vv, tq, tk, tv, vout, tout,
    kbuf, vbuf, qbuf, obuf, tqbuf, tsend, tin,
    local_sem, k_send, k_recv, v_send, v_recv, kf_send, kf_recv, vf_send, vf_recv,
    q_send, q_recv, o_send, o_recv, t_send, t_recv,
):
    rows = vq.shape[0]
    heads = vq.shape[1] // HEAD_DIM
    text = tq.shape[0]
    chips = blk_count * uly_count // CORES
    video_keys = chips * CORES * rows
    text_each = text // (chips * CORES)
    me = lax.axis_index("blk") * uly_count + lax.axis_index("uly")
    core = lax.rem(me, CORES)
    chip = me // CORES
    head = lax.rem(chip, heads)
    base = chip - head

    def device(to_chip, to_core):
        index = to_chip * CORES + to_core
        return (index // uly_count, lax.rem(index, uly_count))

    def columns(index):
        return pl.ds(pl.multiple_of(index * HEAD_DIM, HEAD_DIM), HEAD_DIM)

    def slot(k, of_core):
        return pl.ds(pl.multiple_of((k * CORES + of_core) * rows, rows), rows)

    def row_block(k):
        return pl.ds(pl.multiple_of(k * rows, rows), rows)

    def remote(src, dst, send, recv, target):
        return pltpu.make_async_remote_copy(
            src_ref=src, dst_ref=dst, send_sem=send, recv_sem=recv,
            device_id=target, device_id_type=MESH,
        )

    def kv_copies(k):
        to = pair(chip, k, chips)
        where = columns(lax.rem(to, heads))
        return (
            remote(vk.at[:, where], kbuf.at[slot(k, core), :], k_send.at[k], k_recv.at[k], device(to, core)),
            remote(vv.at[:, where], vbuf.at[slot(k, core), :], v_send.at[k], v_recv.at[k], device(to, core)),
        )

    def forward_copies(k, of_core):
        part = slot(k, of_core)
        return (
            remote(kbuf.at[part, :], kbuf.at[part, :], kf_send.at[k], kf_recv.at[k], device(chip, 1 - core)),
            remote(vbuf.at[part, :], vbuf.at[part, :], vf_send.at[k], vf_recv.at[k], device(chip, 1 - core)),
        )

    def q_copy(k):
        to = pair(head, k, heads)
        return remote(
            vq.at[:, columns(to)], qbuf.at[row_block(k), :], q_send.at[k], q_recv.at[k],
            device(base + to, core),
        )

    def o_copy(k):
        to = pair(head, k, heads)
        return remote(
            obuf.at[row_block(k), :], vout.at[:, columns(head)], o_send.at[k], o_recv.at[k],
            device(base + to, core),
        )

    def t_copy(k):
        to = pair(head, k, heads)
        return remote(tsend.at[k], tin.at[head], t_send.at[k], t_recv.at[k], device(base + to, core))

    text_rows = pl.ds(video_keys, text)
    own = [
        pltpu.make_async_copy(vk.at[:, columns(head)], kbuf.at[slot(0, core), :], local_sem.at[0]),
        pltpu.make_async_copy(vv.at[:, columns(head)], vbuf.at[slot(0, core), :], local_sem.at[1]),
        pltpu.make_async_copy(vq.at[:, columns(head)], qbuf.at[row_block(0), :], local_sem.at[2]),
        pltpu.make_async_copy(tq.at[:, columns(head)], tqbuf, local_sem.at[3]),
        pltpu.make_async_copy(tk.at[:, columns(head)], kbuf.at[text_rows, :], local_sem.at[4]),
        pltpu.make_async_copy(tv.at[:, columns(head)], vbuf.at[text_rows, :], local_sem.at[5]),
    ]
    for copy in own:
        copy.start()

    barrier = pltpu.get_barrier_semaphore()

    def greet(k, _):
        pl.semaphore_signal(
            barrier, inc=1, device_id=device(pair(chip, k, chips), core), device_id_type=MESH
        )
        return 0

    lax.fori_loop(1, chips, greet, 0)
    pl.semaphore_signal(barrier, inc=1, device_id=device(chip, 1 - core), device_id_type=MESH)
    pl.semaphore_wait(barrier, chips)

    def send_kv(j, _):
        k = chips - j
        for copy in kv_copies(k):
            copy.start()
        return 0

    lax.fori_loop(1, chips, send_kv, 0)
    for copy in own:
        copy.wait()
    for copy in forward_copies(0, core):
        copy.start()

    def hand_on(j, _):
        k = chips - j
        for copy in kv_copies(k):
            copy.wait_recv()
        for copy in forward_copies(k, core):
            copy.start()
        if chips == heads:
            q_copy(k).start()
        else:
            pl.when(k < heads)(lambda: q_copy(k).start())
        return 0

    lax.fori_loop(1, chips, hand_on, 0)

    picked = heads * text_each
    shift = text_each.bit_length() - 1
    row = lax.broadcasted_iota(jnp.int32, (picked, text), 0)
    source = lax.broadcasted_iota(jnp.int32, (picked, text), 1)
    k_of = lax.shift_right_logical(row, shift)
    owner = base + lax.bitwise_xor(jnp.full_like(k_of, head), k_of)
    wanted = (owner * CORES + core) * text_each + (row - k_of * text_each)
    pick = jnp.where(source == wanted, 1.0, 0.0).astype(jnp.bfloat16)
    text_queries = jnp.dot(pick, tqbuf[...], preferred_element_type=jnp.float32).astype(jnp.bfloat16)

    def arrive(k, _):
        for copy in forward_copies(k, 1 - core):
            copy.wait_recv()
        return 0

    lax.fori_loop(0, chips, arrive, 0)

    attended = attend(text_queries, kbuf, vbuf, key_width)
    for k in range(heads):
        tsend[k, 0:text_each, :] = attended[k * text_each : (k + 1) * text_each, :]

    def send_text(k, _):
        t_copy(k).start()
        return 0

    lax.fori_loop(1, heads, send_text, 0)
    tin[head, :, :] = tsend[0, :, :]

    home = pltpu.make_async_copy(obuf.at[row_block(0), :], vout.at[:, columns(head)], local_sem.at[0])

    def block(step, _):
        b = heads // group - 1 - step
        for i in range(group):
            k = b * group + i
            if i == 0:
                pl.when(k > 0)(lambda: q_copy(k).wait_recv())
            else:
                q_copy(k).wait_recv()
        here = pl.ds(pl.multiple_of(b * group * rows, group * rows), group * rows)
        obuf[here, :] = attend(qbuf[here, :], kbuf, vbuf, key_width).astype(jnp.bfloat16)
        for i in range(group):
            k = b * group + i
            if i == 0:
                pl.when(k > 0)(lambda: o_copy(k).start())
                pl.when(k == 0)(lambda: home.start())
            else:
                o_copy(k).start()
        return 0

    lax.fori_loop(0, heads // group, block, 0)

    def finish(k, _):
        t_copy(k).wait()
        q_copy(k).wait_send()
        return 0

    lax.fori_loop(1, heads, finish, 0)
    for h in range(heads):
        tout[:, h * HEAD_DIM : (h + 1) * HEAD_DIM] = tin[h, 0:text_each, :].astype(jnp.bfloat16)
    home.wait()

    def finish_kv(k, _):
        for copy in kv_copies(k) + forward_copies(k, core):
            copy.wait_send()
        return 0

    for copy in forward_copies(0, core):
        copy.wait_send()
    lax.fori_loop(1, chips, finish_kv, 0)

    def finish_o(k, _):
        o_copy(k).wait()
        return 0

    lax.fori_loop(1, heads, finish_o, 0)


def hand_over(video, words, video_out, words_out, sem):
    copies = [
        pltpu.make_async_copy(video, video_out, sem.at[0]),
        pltpu.make_async_copy(words, words_out, sem.at[1]),
    ]
    for copy in copies:
        copy.start()
    for copy in copies:
        copy.wait()


def per_device(blk_count, uly_count, video_q, video_k, video_v, text_q, text_k, text_v):
    rows, width = video_q.shape
    heads = width // HEAD_DIM
    text = text_q.shape[0]
    chips = blk_count * uly_count // CORES
    keys = chips * CORES * rows + text
    text_each = text // (chips * CORES)
    tile = max(text_each, 8)
    flops = 4 * (heads * rows + heads * text_each) * keys * HEAD_DIM
    dma = pltpu.SemaphoreType.DMA
    any_space = pl.BlockSpec(memory_space=pl.ANY)
    video, words = pl.pallas_call(
        functools.partial(kernel, blk_count, uly_count, 2176, 4),
        out_shape=(
            jax.ShapeDtypeStruct((rows, width), jnp.bfloat16),
            jax.ShapeDtypeStruct((text_each, width), jnp.bfloat16),
        ),
        in_specs=[any_space] * 6,
        out_specs=(pl.BlockSpec(memory_space=pltpu.VMEM), pl.BlockSpec(memory_space=pltpu.VMEM)),
        scratch_shapes=[
            pltpu.VMEM((keys, HEAD_DIM), jnp.bfloat16),
            pltpu.VMEM((keys, HEAD_DIM), jnp.bfloat16),
            pltpu.VMEM((heads * rows, HEAD_DIM), jnp.bfloat16),
            pltpu.VMEM((heads * rows, HEAD_DIM), jnp.bfloat16),
            pltpu.VMEM((text, HEAD_DIM), jnp.bfloat16),
            pltpu.VMEM((heads, tile, HEAD_DIM), jnp.float32),
            pltpu.VMEM((heads, tile, HEAD_DIM), jnp.float32),
            dma((6,)),
        ]
        + [dma((chips,))] * 8
        + [dma((heads,))] * 6,
        compiler_params=pltpu.CompilerParams(
            collective_id=0, has_side_effects=True, vmem_limit_bytes=56 * 1024 * 1024
        ),
        cost_estimate=pl.CostEstimate(
            flops=flops, bytes_accessed=8 * rows * width * 2, transcendentals=flops // (4 * HEAD_DIM)
        ),
    )(video_q, video_k, video_v, text_q, text_k, text_v)
    return pl.pallas_call(
        hand_over,
        out_shape=(
            jax.ShapeDtypeStruct(video.shape, video.dtype),
            jax.ShapeDtypeStruct(words.shape, words.dtype),
        ),
        in_specs=[pl.BlockSpec(memory_space=pltpu.VMEM)] * 2,
        out_specs=(any_space,) * 2,
        scratch_shapes=[dma((2,))],
    )(video, words)


def solution(mesh):
    rows = P(("blk", "uly"), None)
    return jax.shard_map(
        functools.partial(per_device, mesh.shape["blk"], mesh.shape["uly"]),
        mesh=mesh,
        in_specs=(rows, rows, rows, P(), P(), P()),
        out_specs=(rows, rows),
        check_vma=False,
    )
```
